512 devices in a mesh: dp: 8 (over x, y_lo), expert: 64 (over y_hi, z, core).
Axes of the slice: x: 4, y: 8 (y_hi: 4, y_lo: 2; y = y_hi * 2 + y_lo), z: 8, core: 2. Of those that a mesh axis runs over, the one named last changes fastest.
Arguments:
- codes: bfloat16 [4096, 7168], P(('dp', 'expert')), may hold values from -6 to 6
- exponents: int32 [4096, 56], P(('dp', 'expert')), may hold values from -2 to 1
- routes: int32 [4096, 8], P(('dp', 'expert')), may hold values from 0 to 63, all different within a row; in each aligned block of 8 rows (0 to 7, 8 to 15, ...) at most 2 rows name the same one
- gate_weight: bfloat16 [64, 7168, 1024], P('expert', None, 'dp'), may hold values from -0.0625 to 0.0625
- up_weight: bfloat16 [64, 7168, 1024], P('expert', None, 'dp'), may hold values from -0.0625 to 0.0625
Outputs:
- hidden: bfloat16 [64, 1024, 1024], P('expert', None, 'dp')
- hessians: float32 [64, 1024, 1024], P('expert', 'dp')
The draws below stay inside these ranges and needn't reach their ends.
Inputs may be any that keep to these rules, and one draw needn't show every extreme that they name: `routes`: each row names 8 different experts; among the 8 rows of one device no expert is named more than 2 times, and in every draw some expert is named exactly 2 times by the rows of some device.
All inputs are finite; a program needn't handle non-finite values.
Results may differ from the reference program's by a relative error of at most 0.0046.
Values may be sent and summed in bfloat16 or wider, within the bound.
A program may use at most 128 MiB of HBM per device.

```python
import math
import jax
import jax.numpy as jnp
import numpy as np
from jax import lax

D = 7168
FF = 1024
TOP = 8
TOK_DEV = 8
EXPERTS = 64
CAP = 2
TOKENS = 4096


def touch_ends(drawn, stream_key, least, high):
    index_at = [jax.random.randint(jax.random.fold_in(stream_key, axis), (), 0, length) for axis, length in enumerate(drawn.shape)]
    longest = drawn.shape.index(max(drawn.shape))
    beside = index_at[:longest] + [(index_at[longest] + 1) % drawn.shape[longest]] + index_at[longest + 1:]
    return drawn.at[tuple(index_at)].set(least).at[tuple(beside)].set(high)


def block_scale(own_key, shape, split, least, top_value):
    gain, own = 1.0, jax.random.fold_in(own_key, 6)
    for dim, parts in split:
        steps = jnp.exp(jax.random.uniform(jax.random.fold_in(own, dim), (parts,), jnp.float32, least / len(split), top_value / len(split)))
        gain = gain * jnp.repeat(steps, shape[dim] // parts).reshape([-1 if axis == dim else 1 for axis in range(len(shape))])
    return gain


def routed_block(stream_key, own, number, rows, amount, top, most, lean):
    ranking = jax.random.permutation(stream_key, amount)
    crowded, common = portions_of(amount, rows * top, most, lean, True), portions_of(amount, rows * top, most, lean, False)
    places = jnp.arange(amount)

    def named(sizes, rotation):
        used = int((sizes > 0).sum())
        fixed = max(1, used // 4)
        passed = fixed + (places - fixed + rotation * (used - fixed)) % max(1, amount - fixed)
        return jnp.zeros((amount,), jnp.int32).at[ranking[jnp.where(places < fixed, places, passed)]].set(jnp.asarray(sizes, jnp.int32))

    sizes = jnp.where(number % 4 == 0, named(crowded, number // 4), named(common, number - number // 4 - 1))
    mixed = jax.random.permutation(jax.random.fold_in(own, 3), amount)
    source_of, receiver = mixed[0:amount // 2 * 2:2], mixed[1:amount // 2 * 2:2]
    slack = jnp.minimum(sizes[source_of] - 1, most - sizes[receiver]) // 2
    slack = jnp.where((source_of == ranking[0]) | (receiver == ranking[0]) | (sizes[receiver] == 0), 0, jnp.maximum(slack, 0))
    passed = jax.random.randint(jax.random.fold_in(own, 4), (amount // 2,), 0, 1 << 20) % (slack + 1)
    sizes = sizes.at[source_of].add(-passed).at[receiver].add(passed)
    members = jnp.searchsorted(jnp.cumsum(sizes), jnp.arange(rows * top), side="right").astype(jnp.int32)
    grid = members.reshape(top, rows).T
    grid = grid[jax.random.permutation(jax.random.fold_in(own, 1), rows)]
    rotation = jax.random.randint(jax.random.fold_in(own, 2), (rows, 1), 0, top)
    return jnp.take_along_axis(grid, (jnp.arange(top)[None, :] + rotation) % top, axis=1)


def portions_of(count, total, limit, slope, full):
    loads = [(1 << 20) // math.isqrt(standing ** slope) + 1 for standing in range(1, count + 1)]
    largest = limit if full else min(limit, max(-(-total // count), total * loads[0] // sum(loads)))
    least = 1 if total - largest >= count - 1 else 0
    given, spare = [largest] + [least] * (count - 1), total - largest - least * (count - 1)
    while spare > 0:
        free = [i for i in range(1, count) if given[i] < largest] or [i for i in range(1, count) if given[i] < limit]
        mass, remaining = sum([loads[i] for i in free]), spare
        for i in free:
            extra = min(limit - given[i], max(1, remaining * loads[i] // mass), spare)
            given[i] = given[i] + extra
            spare = spare - extra
    return np.array(given)


def centred(key, extent, scale, limit, pieces=(), kind=jnp.bfloat16):
    array = scale * jax.random.normal(key, extent, jnp.float32)
    if pieces:
        array = array * block_scale(key, extent, pieces, -0.22, 0.18)
    return jnp.clip(array, -limit, limit).astype(kind)


def setup_inputs(seed: int = 0) -> dict:
    key_of = jax.random.split(jax.random.key(seed), 6)
    codes = centred(key_of[0], (TOKENS, D), 1.0, 6.0, ((0, 512),))
    exponents = touch_ends(jax.random.randint(key_of[1], (TOKENS, D // 128), -2, 2), jax.random.fold_in(key_of[1], 1), -2, 1).astype(jnp.int32)
    routes_keys = jax.random.split(jax.random.fold_in(key_of[2], 1), TOKENS // TOK_DEV)
    routes_turns = jax.random.permutation(jax.random.fold_in(key_of[2], 3), TOKENS // TOK_DEV)
    routes = jax.vmap(lambda own, number: routed_block(jax.random.fold_in(key_of[2], 2), own, number, TOK_DEV, EXPERTS, TOP, CAP, 0))(routes_keys, routes_turns).reshape((TOKENS, TOP))
    gate_weight = centred(key_of[3], (EXPERTS, D, FF), D ** -0.5, 0.0625, ((0, 64), (2, 8)))
    up_weight = centred(key_of[4], (EXPERTS, D, FF), D ** -0.5, 0.0625, ((0, 64), (2, 8)))
    return {"codes": codes, "exponents": exponents, "routes": routes, "gate_weight": gate_weight, "up_weight": up_weight}


def dequantize(codes, exponents):
    scale_full = jnp.zeros(exponents.shape, jnp.float32)
    for exponent_value in range(-2, 2):
        scale_full = scale_full + jnp.where(exponents == exponent_value, 2.0 ** exponent_value, 0.0).astype(jnp.float32)
    block_count = codes.shape[1] // 128
    scaled = codes.reshape(codes.shape[0], block_count, 128) * scale_full.astype(jnp.bfloat16)[:, :, None]
    return scaled.reshape(codes.shape)


def slot_matrix(routes, expert_count, capacity):
    chosen = (routes[:, :, None] == jnp.arange(expert_count, dtype=jnp.int32)[None, None, :]).astype(jnp.int32)
    counts = jnp.sum(chosen, axis=1)
    earlier = jnp.cumsum(counts, axis=0) - counts
    position = jnp.sum(chosen * earlier[:, None, :], axis=2)
    slot_hot = (position[:, :, None] == jnp.arange(capacity, dtype=jnp.int32)[None, None, :]).astype(jnp.float32)
    matrix = jnp.einsum("tke,tkc->ect", chosen.astype(jnp.float32), slot_hot)
    return matrix.astype(jnp.bfloat16)


def reference(codes, exponents, routes, gate_weight, up_weight):
    tokens = dequantize(codes, exponents)
    expert_count = gate_weight.shape[0]
    sources = codes.shape[0] // TOK_DEV

    def source_matrix(source_routes):
        return slot_matrix(source_routes, expert_count, CAP)

    matrices = jax.vmap(source_matrix)(routes.reshape(sources, TOK_DEV, TOP))
    per_expert = jnp.transpose(matrices, (1, 0, 2, 3))
    blocks = tokens.reshape(sources, TOK_DEV, -1).astype(jnp.float32)
    weight_scale = 1.0 / (codes.shape[0] * TOP // expert_count)

    def one_expert(inputs):
        matrix, gate_local, up_local = inputs
        slot_rows = jnp.einsum("qct,qtd->qcd", matrix.astype(jnp.float32), blocks).astype(jnp.bfloat16)
        slot_rows = slot_rows.reshape(-1, slot_rows.shape[-1])
        gate_part = jnp.dot(slot_rows, gate_local, preferred_element_type=jnp.float32)
        up_part = jnp.dot(slot_rows, up_local, preferred_element_type=jnp.float32)
        activations = (jax.nn.silu(gate_part) * up_part).astype(jnp.bfloat16)
        moment = lax.dot_general(activations, activations, (((0,), (0,)), ((), ())), preferred_element_type=jnp.float32)
        return activations, moment * weight_scale

    hidden, hessians = lax.map(one_expert, (per_expert, gate_weight, up_weight))
    return hidden, hessians
```

```python
import functools

import jax
import jax.numpy as jnp
from jax import lax
from jax.experimental import pallas as pl
from jax.experimental.pallas import tpu as pltpu
from jax.sharding import PartitionSpec as P

MESH = pl.DeviceIdType.MESH
F32 = jnp.float32
BF16 = jnp.bfloat16

NX, NY, NZ = 4, 8, 8
TOK = 8
D = 7168
HALF = D // 2
LANES = 128
NC = 4
BLK = HALF // LANES
CB = BLK // NC
KC = CB * LANES
NH = 2
RB = 16
HR = NZ * RB
SL = NX * HR
FB = 128


def kernel(
    scale_out,
    codes,
    exponents,
    routes,
    gate_w,
    up_w,
    hidden_out,
    hess_out,
    deq,
    table,
    deq_in,
    table_in,
    tok,
    sel,
    zsend,
    rows,
    wbuf,
    acc,
    part,
    hall,
    hperm,
    hess,
    core_s,
    core_r,
    y_s,
    y_r,
    z_s,
    z_r,
    x_s,
    x_r,
    w_s,
    w_r,
    p_s,
    p_r,
    hx_s,
    hx_r,
    hc_s,
    hc_r,
    f_s,
    f_r,
):
    dp = lax.axis_index("dp")
    ex = lax.axis_index("expert")
    x, l = dp // 2, dp % 2
    yh, z, c = ex // (2 * NZ), (ex // 2) % NZ, ex % 2
    y = yh * 2 + l
    o = 1 - c
    xr, xl, xo = (x + 1) % NX, (x + 3) % NX, (x + 2) % NX

    def dev(dx, dy, dz, dc):
        return (dx * 2 + dy % 2, ((dy // 2) * NZ + dz) * 2 + dc)

    def remote(src, dst, send, recv, to):
        return pltpu.make_async_remote_copy(
            src_ref=src, dst_ref=dst, send_sem=send, recv_sem=recv, device_id=to, device_id_type=MESH
        )

    other_core = dev(x, y, z, o)
    y_pair = yh * 2 + (1 - l)

    barrier = pltpu.get_barrier_semaphore()

    def greet(to):
        pl.semaphore_signal(barrier, inc=1, device_id=to, device_id_type=MESH)

    def greet_ring(j, carry):
        greet(dev(x, (y + j) % NY, z, c))
        greet(dev(x, y, (z + j) % NZ, c))
        return carry

    greet(other_core)
    greet(dev(x, y_pair, z, o))
    greet(dev(xr, y, z, c))
    greet(dev(xl, y, z, c))
    lax.fori_loop(1, NY, greet_ring, 0)

    ev = exponents[...]
    scale = jnp.zeros(ev.shape, F32)
    for e in range(-2, 2):
        scale = jnp.where(ev == e, jnp.float32(2.0**e), scale)
    for b in range(2 * BLK):
        deq[b] = codes[:, b * LANES : (b + 1) * LANES].astype(F32) * scale[:, b : b + 1]
    rv = routes[...]
    lane = lax.broadcasted_iota(jnp.int32, (TOK, LANES), 1)
    chosen = jnp.zeros((TOK, LANES), F32)
    for t in range(rv.shape[1]):
        chosen = jnp.where(rv[:, t : t + 1] == lane, 1.0, chosen)
    row = lax.broadcasted_iota(jnp.int32, (TOK, LANES), 0)
    order = chosen
    for t in range(TOK - 1):
        order = order + jnp.where(row > t, chosen[t : t + 1, :], 0.0)
    table[...] = chosen * order

    pl.semaphore_wait(barrier, 18)

    def core_copy(n):
        if n == 0:
            return remote(deq.at[pl.ds(o * BLK, BLK)], deq_in, core_s.at[0], core_r.at[0], other_core)
        return remote(table, table_in, core_s.at[1], core_r.at[1], other_core)

    for n in range(2):
        core_copy(n).start()
    for n in range(2):
        core_copy(n).wait_recv()

    def pack(own, oth):
        return jnp.concatenate([jnp.where(c == 0, own, oth), jnp.where(c == 0, oth, own)], axis=0).astype(BF16)

    tok[y, 0] = pack(table[...], table_in[...])

    def assemble(j, carry):
        tok[y, 1 + j] = pack(deq[c * BLK + j], deq_in[j])
        return carry

    lax.fori_loop(0, BLK, assemble, 0)

    def chunk_blocks(k):
        first = 0 if k == 0 else 1 + k * CB
        return pl.ds(first, 1 + (k + 1) * CB - first)

    def y_copy(k, src_y, dst_y):
        part_ref = tok.at[src_y, chunk_blocks(k)]
        return remote(part_ref, part_ref, y_s.at[k, dst_y], y_r.at[k, src_y], dev(x, dst_y, z, c))

    def ring(n, me, act):
        def body(j, carry):
            act((me + j) % n)
            return carry

        lax.fori_loop(1, n, body, 0)

    for k in range(NC):
        ring(NY, y, lambda to, k=k: y_copy(k, y, to).start())

    def w_copy(k, d, m):
        src = (gate_w, up_w)[m].at[pl.ds(d * HALF + k * KC, KC)]
        dst = wbuf.at[k, l * 2 + m]
        return remote(src, dst, w_s.at[k, d, m], w_r.at[k, l * 2 + m], dev(x, yh * 2 + c, z, d))

    def w_local(k, m):
        src = (gate_w, up_w)[m].at[pl.ds(c * HALF + k * KC, KC)]
        return pltpu.make_async_copy(src, wbuf.at[k, l * 2 + m], w_r.at[k, l * 2 + m])

    def w_start(k):
        for m in range(2):
            for d in range(2):
                @pl.when(jnp.logical_or(c != l, c != d))
                def _():
                    w_copy(k, d, m).start()

            @pl.when(c == l)
            def _():
                w_local(k, m).start()

    def w_wait_recv(k):
        for j in range(4):
            pltpu.make_async_copy(wbuf.at[k, j], wbuf.at[k, j], w_r.at[k, j]).wait()

    def w_wait_send(k):
        for m in range(2):
            for d in range(2):
                @pl.when(jnp.logical_or(c != l, c != d))
                def _():
                    w_copy(k, d, m).wait_send()

    def build_selection():
        r = lax.broadcasted_iota(jnp.int32, (NH * HR, LANES), 0)
        q = lax.broadcasted_iota(jnp.int32, (NH * HR, LANES), 1)
        expert = (yh * NZ + (r // RB) % NZ) * 2 + l
        wanted = jnp.where(q == expert, 1.0, 0.0).astype(BF16)
        names = tok[:, 0].reshape(NY * 2 * TOK, LANES)
        place = lax.dot_general(wanted, names, (((1,), (1,)), ((), ())), preferred_element_type=F32)
        r16 = r % RB
        source = ((r // HR) * (NY // NH) + r16 // 4) * 2 + (r16 // 2) % 2
        hit = jnp.logical_and(place == (r16 % 2 + 1).astype(F32), q // TOK == source)
        sel[...] = jnp.where(hit, 1.0, 0.0).astype(BF16).reshape(NH, HR, LANES)

    def z_copy(h, k, src_z, dst_z):
        return remote(
            zsend.at[h, k, dst_z],
            rows.at[h, k, x, src_z],
            z_s.at[h, k, dst_z],
            z_r.at[h, k, src_z],
            dev(x, y, dst_z, c),
        )

    def stage_a(h, k):
        if h == 0:
            ring(NY, y, lambda fr: y_copy(k, fr, fr).wait_recv())
        if h == 0 and k == 0:
            build_selection()
        for j in range(CB):
            names = tok[:, 1 + k * CB + j].reshape(NY * 2 * TOK, LANES)
            got = jnp.dot(sel[h], names, preferred_element_type=F32).astype(BF16)
            zsend[h, k, :, :, j * LANES : (j + 1) * LANES] = got.reshape(NZ, RB, LANES)
        ring(NZ, z, lambda to: z_copy(h, k, z, to).start())
        rows[h, k, x, z] = zsend[h, k, z]

    def x_copy(h, k, n):
        if n == 0:
            ref, to = rows.at[h, k, x], xr
        elif n == 1:
            ref, to = rows.at[h, k, x], xl
        elif n == 2:
            ref, to = rows.at[h, k, xl, pl.ds(0, NZ // 2)], xr
        else:
            ref, to = rows.at[h, k, xr, pl.ds(NZ // 2, NZ // 2)], xl
        return remote(ref, ref, x_s.at[h, k, n], x_r.at[h, k, n], dev(to, y, z, c))

    def x_wait(h, k, n):
        if n == 0:
            ref = rows.at[h, k, xl]
        elif n == 1:
            ref = rows.at[h, k, xr]
        elif n == 2:
            ref = rows.at[h, k, xo, pl.ds(0, NZ // 2)]
        else:
            ref = rows.at[h, k, xo, pl.ds(NZ // 2, NZ // 2)]
        remote(ref, ref, x_s.at[h, k, n], x_r.at[h, k, n], dev(xr, y, z, c)).wait_recv()

    def stage_b(h, k):
        ring(NZ, z, lambda fr: z_copy(h, k, fr, fr).wait_recv())
        x_copy(h, k, 0).start()
        x_copy(h, k, 1).start()

    def stage_c(h, k):
        x_wait(h, k, 0)
        x_copy(h, k, 2).start()
        x_wait(h, k, 1)
        x_copy(h, k, 3).start()

    def stage_d(h, k):
        if h == 0:
            w_wait_recv(k)
        x_wait(h, k, 2)
        x_wait(h, k, 3)

        def body(i, carry):
            left = rows[h, k, pl.ds(2 * i, 2)].reshape(2 * HR, KC)
            for s in range(2):
                right = jnp.concatenate([wbuf[k, 2 * s], wbuf[k, 2 * s + 1]], axis=1)
                got = jnp.dot(left, right, preferred_element_type=F32)
                at = pl.ds(pl.multiple_of(i * 2 * HR, 2 * HR), 2 * HR)
                if k == 0:
                    acc[h, s, at] = got
                else:
                    acc[h, s, at] = acc[h, s, at] + got
            return carry

        lax.fori_loop(0, NX // 2, body, 0)
        if k == NC - 1:
            p_copy(h).start()

    def p_copy(h):
        return remote(acc.at[h, o], part.at[h], p_s.at[h], p_r.at[h], other_core)

    def finish_hidden(h):
        p_copy(h).wait_recv()

        def body(i, carry):
            at = pl.ds(pl.multiple_of(i * HR, HR), HR)
            both = acc[h, c, at] + part[h, at]
            gate, up = both[:, :FB], both[:, FB:]
            value = (gate / (1.0 + jnp.exp(-gate)) * up).astype(BF16)
            hall[h, x, c, at] = value
            return carry

        lax.fori_loop(0, NX, body, 0)
        hx_copy(h, 0).start()
        hx_copy(h, 1).start()
        hc_copy(h, 0).start()

        r = lax.broadcasted_iota(jnp.int32, (HR, HR), 0)
        q = lax.broadcasted_iota(jnp.int32, (HR, HR), 1)
        origin = ((r // 4) % 8) * RB + (((r // 32) % 2) * 2 + r // 64) * 4 + r % 4
        turn = jnp.where(q == origin, 1.0, 0.0).astype(BF16)

        def place(i, carry):
            block = hall[h, x, c, pl.ds(pl.multiple_of(i * HR, HR), HR)]
            got = jnp.dot(turn, block, preferred_element_type=F32).astype(BF16)
            for s in range(2):
                at = pl.multiple_of(i * 2 * HR + s * HR + h * 64, 64)
                hperm[pl.ds(at, 64)] = got[s * 64 : (s + 1) * 64]
            return carry

        lax.fori_loop(0, NX, place, 0)

    def hx_copy(h, n):
        if n == 0:
            ref, to = hall.at[h, x, c], xr
        elif n == 1:
            ref, to = hall.at[h, x, c], xl
        elif n == 2:
            ref, to = hall.at[h, xl, c, pl.ds(0, SL // 2)], xr
        else:
            ref, to = hall.at[h, xr, c, pl.ds(SL // 2, SL // 2)], xl
        return remote(ref, ref, hx_s.at[h, n], hx_r.at[h, n], dev(to, y, z, c))

    def hx_wait(h, n):
        if n == 0:
            ref = hall.at[h, xl, c]
        elif n == 1:
            ref = hall.at[h, xr, c]
        elif n == 2:
            ref = hall.at[h, xo, c, pl.ds(0, SL // 2)]
        else:
            ref = hall.at[h, xo, c, pl.ds(SL // 2, SL // 2)]
        remote(ref, ref, hx_s.at[h, n], hx_r.at[h, n], dev(xr, y, z, c)).wait_recv()

    def hc_copy(h, n):
        ref = hall.at[h, (x, xl, xr, xo)[n], c]
        return remote(ref, ref, hc_s.at[h, n], hc_r.at[h, n], other_core)

    def hc_wait(h, n):
        ref = hall.at[h, (x, xl, xr, xo)[n], o]
        remote(ref, ref, hc_s.at[h, n], hc_r.at[h, n], other_core).wait_recv()

    def relay_hidden(h):
        hx_wait(h, 0)
        hx_copy(h, 2).start()
        hc_copy(h, 1).start()
        hx_wait(h, 1)
        hx_copy(h, 3).start()
        hc_copy(h, 2).start()

    def last_hidden(h):
        hx_wait(h, 2)
        hx_wait(h, 3)
        hc_copy(h, 3).start()

    def hess_part(h, n):
        hc_wait(h, n)
        at = (x, xl, xr, xo)[n]
        right = jnp.concatenate([hall[h, at, 0], hall[h, at, 1]], axis=1)
        got = lax.dot_general(hall[h, x, c], right, (((0,), (0,)), ((), ())), preferred_element_type=F32)
        if h == 0:
            hess[at] = got
        else:
            hess[at] = (hess[at] + got) * scale_out

    steps = [(h, k) for h in range(NH) for k in range(NC)]
    stage_a(*steps[0])
    w_start(0)
    stage_a(*steps[1])
    w_start(1)
    stage_b(*steps[0])
    stage_a(*steps[2])
    w_start(2)
    stage_b(*steps[1])
    stage_c(*steps[0])
    stage_a(*steps[3])
    w_start(3)
    stage_b(*steps[2])
    stage_c(*steps[1])
    stage_a(*steps[4])
    stage_b(*steps[3])
    stage_c(*steps[2])
    stage_d(*steps[0])
    stage_a(*steps[5])
    stage_b(*steps[4])
    stage_c(*steps[3])
    stage_d(*steps[1])
    stage_a(*steps[6])
    stage_b(*steps[5])
    stage_c(*steps[4])
    stage_a(*steps[7])
    stage_d(*steps[2])
    stage_b(*steps[6])
    stage_c(*steps[5])
    stage_d(*steps[3])
    stage_b(*steps[7])
    stage_d(*steps[4])
    stage_c(*steps[6])
    finish_hidden(0)
    stage_d(*steps[5])
    stage_c(*steps[7])
    relay_hidden(0)
    stage_d(*steps[6])
    stage_d(*steps[7])
    last_hidden(0)
    for n in range(4):
        hess_part(0, n)
    finish_hidden(1)
    relay_hidden(1)
    hess_part(1, 0)
    last_hidden(1)

    owner = dev(x, yh * 2 + c, z, l)

    def out_remote(n):
        if n == 0:
            return remote(hperm, hidden_out, f_s.at[0], f_r.at[0], owner)
        return remote(hess.at[n - 1], hess_out.at[n - 1], f_s.at[n], f_r.at[n], owner)

    def out_local(n):
        if n == 0:
            return pltpu.make_async_copy(hperm, hidden_out, f_r.at[0])
        return pltpu.make_async_copy(hess.at[n - 1], hess_out.at[n - 1], f_r.at[n])

    def out_start(n):
        @pl.when(c != l)
        def _():
            out_remote(n).start()

        @pl.when(c == l)
        def _():
            out_local(n).start()

    out_start(0)
    for n in range(1, 4):
        hess_part(1, n)
    for n in range(NX):
        out_start(1 + n)

    for n in range(2):
        core_copy(n).wait_send()
    for k in range(NC):
        ring(NY, y, lambda to, k=k: y_copy(k, y, to).wait_send())
        w_wait_send(k)
    for h, k in steps:
        ring(NZ, z, lambda to, h=h, k=k: z_copy(h, k, z, to).wait_send())
        for n in range(4):
            x_copy(h, k, n).wait_send()
    for h in range(NH):
        p_copy(h).wait_send()
        for n in range(4):
            hx_copy(h, n).wait_send()
            hc_copy(h, n).wait_send()
    for n in range(5):
        @pl.when(c != l)
        def _():
            out_remote(n).wait_send()
        if n == 0:
            pltpu.make_async_copy(hperm, hidden_out, f_r.at[0]).wait()
        else:
            pltpu.make_async_copy(hess.at[n - 1], hess_out.at[n - 1], f_r.at[n]).wait()


def shards(codes, exponents, routes, gate_weight, up_weight):
    sem = pltpu.SemaphoreType.DMA
    vmem = pl.BlockSpec(memory_space=pltpu.VMEM)
    hbm = pl.BlockSpec(memory_space=pl.ANY)
    scale_out = 1.0 / (TOK * NX * NY * NZ * 2 * routes.shape[1] // (NY * NZ))
    hidden, hess = pl.pallas_call(
        functools.partial(kernel, scale_out),
        out_shape=(
            jax.ShapeDtypeStruct((NH * SL, FB), BF16),
            jax.ShapeDtypeStruct((NX, FB, 2 * FB), F32),
        ),
        in_specs=[vmem, vmem, vmem, hbm, hbm],
        out_specs=(hbm, hbm),
        scratch_shapes=[
            pltpu.VMEM((2 * BLK, TOK, LANES), F32),
            pltpu.VMEM((TOK, LANES), F32),
            pltpu.VMEM((BLK, TOK, LANES), F32),
            pltpu.VMEM((TOK, LANES), F32),
            pltpu.VMEM((NY, 1 + BLK, 2 * TOK, LANES), BF16),
            pltpu.VMEM((NH, HR, LANES), BF16),
            pltpu.VMEM((NH, NC, NZ, RB, KC), BF16),
            pltpu.VMEM((NH, NC, NX, NZ, RB, KC), BF16),
            pltpu.VMEM((NC, 4, KC, FB), BF16),
            pltpu.VMEM((NH, 2, SL, 2 * FB), F32),
            pltpu.VMEM((NH, SL, 2 * FB), F32),
            pltpu.VMEM((NH, NX, 2, SL, FB), BF16),
            pltpu.VMEM((NH * SL, FB), BF16),
            pltpu.VMEM((NX, FB, 2 * FB), F32),
            sem((2,)),
            sem((2,)),
            sem((NC, NY)),
            sem((NC, NY)),
            sem((NH, NC, NZ)),
            sem((NH, NC, NZ)),
            sem((NH, NC, 4)),
            sem((NH, NC, 4)),
            sem((NC, 2, 2)),
            sem((NC, 4)),
            sem((NH,)),
            sem((NH,)),
            sem((NH, 4)),
            sem((NH, 4)),
            sem((NH, 4)),
            sem((NH, 4)),
            sem((5,)),
            sem((5,)),
        ],
        compiler_params=pltpu.CompilerParams(
            collective_id=0, has_side_effects=True, vmem_limit_bytes=48 * 1024 * 1024
        ),
        name="routed_stats",
    )(codes, exponents, routes, gate_weight[0], up_weight[0])
    hess = jnp.transpose(hess, (1, 0, 2)).reshape(FB, NX * 2 * FB)
    return hidden[None], hess[None]


def solution(mesh):
    placed = (
        P(("dp", "expert"), None),
        P(("dp", "expert"), None),
        P(("dp", "expert"), None),
        P("expert", None, "dp"),
        P("expert", None, "dp"),
    )
    return jax.shard_map(
        shards,
        mesh=mesh,
        in_specs=placed,
        out_specs=(P("expert", None, "dp"), P("expert", "dp", None)),
        check_vma=False,
    )
```

```python
import functools

import jax
import jax.numpy as jnp
from jax import lax
from jax.experimental import pallas as pl
from jax.experimental.pallas import tpu as pltpu
from jax.sharding import PartitionSpec as P

MESH = pl.DeviceIdType.MESH
F32 = jnp.float32
BF16 = jnp.bfloat16

NX, NY, NZ = 4, 8, 8
TOK = 8
D = 7168
HALF = D // 2
LANES = 128
BLK = HALF // LANES
CUT = 15
NH = 2
RB = 16
CR = NX * NH * RB
SL = NZ * CR
FB = 128
KC = 512
ORDER = (0, 1, 7, 2, 6, 3, 5, 4)
GROUPS = ((0, 4), (4, 6), (6, 8))
PIECES = [(0, 0), (1, 0), (2, 0), (0, 1)] + [(j, 0) for j in range(3, NZ)] + [(j, 1) for j in range(1, NZ)]


def rank_of(distance):
    rank = jnp.zeros_like(distance)
    for j, d in enumerate(ORDER):
        rank = jnp.where(distance == d, j, rank)
    return rank


def kernel(
    scale_out,
    codes_in,
    exponents_in,
    routes_in,
    gate_w,
    up_w,
    hidden_out,
    hess_out,
    codes,
    exponents,
    routes,
    deq,
    table,
    deq_in,
    table_in,
    tok,
    sel,
    zsend,
    rows,
    wbuf,
    acc,
    part,
    hall,
    hown,
    hperm,
    hess,
    in_s,
    core_s,
    core_r,
    y_s,
    y_r,
    z_s,
    z_r,
    x_s,
    x_r,
    w_s,
    w_r,
    p_s,
    p_r,
    hx_s,
    hx_r,
    hc_s,
    hc_r,
    ho_s,
    ho_r,
    f_s,
    f_r,
):
    dp = lax.axis_index("dp")
    ex = lax.axis_index("expert")
    x, l = dp // 2, dp % 2
    yh, z, c = ex // (2 * NZ), (ex // 2) % NZ, ex % 2
    y = yh * 2 + l
    o = 1 - c
    xr, xl, xo = (x + 1) % NX, (x + 3) % NX, (x + 2) % NX
    yr, yl = (y + 1) % NY, (y + NY - 1) % NY

    def dev(dx, dy, dz, dc):
        return (dx * 2 + dy % 2, ((dy // 2) * NZ + dz) * 2 + dc)

    def remote(src, dst, send, recv, to):
        return pltpu.make_async_remote_copy(
            src_ref=src, dst_ref=dst, send_sem=send, recv_sem=recv, device_id=to, device_id_type=MESH
        )

    def ring(n, act):
        def body(j, carry):
            act(j)
            return carry

        lax.fori_loop(1, n, body, 0)

    other_core = dev(x, y, z, o)
    y_pair = yh * 2 + (1 - l)

    inputs = [
        pltpu.make_async_copy(routes_in, routes, in_s.at[0]),
        pltpu.make_async_copy(exponents_in, exponents, in_s.at[1]),
        pltpu.make_async_copy(codes_in, codes, in_s.at[2]),
    ]
    for copy in inputs:
        copy.start()

    barrier = pltpu.get_barrier_semaphore()

    def greet(to):
        pl.semaphore_signal(barrier, inc=1, device_id=to, device_id_type=MESH)

    greet(other_core)
    greet(dev(x, y_pair, z, o))
    greet(dev(x, yr, z, c))
    greet(dev(x, yl, z, c))
    greet(dev(xr, y, z, c))
    greet(dev(xl, y, z, c))
    ring(NZ, lambda j: greet(dev(x, y, (z + j) % NZ, c)))

    inputs[0].wait()
    rv = routes[...]
    lane = lax.broadcasted_iota(jnp.int32, (TOK, LANES), 1)
    chosen = jnp.zeros((TOK, LANES), F32)
    for t in range(rv.shape[1]):
        chosen = jnp.where(rv[:, t : t + 1] == lane, 1.0, chosen)
    row = lax.broadcasted_iota(jnp.int32, (TOK, LANES), 0)
    order = chosen
    for t in range(TOK - 1):
        order = order + jnp.where(row > t, chosen[t : t + 1, :], 0.0)
    table[...] = chosen * order
    inputs[1].wait()
    inputs[2].wait()
    ev = exponents[...]
    scale = jnp.zeros(ev.shape, F32)
    for e in range(-2, 2):
        scale = jnp.where(ev == e, jnp.float32(2.0**e), scale)
    for b in range(2 * BLK):
        deq[b] = codes[:, b * LANES : (b + 1) * LANES].astype(F32) * scale[:, b : b + 1]

    pl.semaphore_wait(barrier, 13)

    def core_copy(n):
        if n == 0:
            return remote(deq.at[pl.ds(o * BLK, BLK)], deq_in, core_s.at[0], core_r.at[0], other_core)
        return remote(table, table_in, core_s.at[1], core_r.at[1], other_core)

    for n in range(2):
        core_copy(n).start()
    for n in range(2):
        core_copy(n).wait_recv()

    def pack(own, oth):
        return jnp.concatenate([jnp.where(c == 0, own, oth), jnp.where(c == 0, oth, own)], axis=0).astype(BF16)

    tok[y, 0] = pack(table[...], table_in[...])

    def assemble(j, carry):
        tok[y, 1 + j] = pack(deq[c * BLK + j], deq_in[j])
        return carry

    lax.fori_loop(0, BLK, assemble, 0, unroll=4)

    def y_ref(src_y, piece):
        return tok.at[src_y, pl.ds(0, CUT) if piece == 0 else pl.ds(CUT, 1 + BLK - CUT)]

    def y_send(step, way, piece):
        src = (y + NY - step) % NY if way == 0 else (y + step) % NY
        to = yr if way == 0 else yl
        ref = y_ref(src, piece)
        return remote(ref, ref, y_s.at[step, way, piece], y_r.at[step, way, piece], dev(x, to, z, c))

    def y_wait(step, way, piece):
        src = (y + NY - step - 1) % NY if way == 0 else (y + step + 1) % NY
        ref = y_ref(src, piece)
        remote(ref, ref, y_s.at[step, way, piece], y_r.at[step, way, piece], dev(x, yr, z, c)).wait_recv()

    y_all = [(step, way, piece) for step in range(4) for piece in range(2) for way in range(2) if step < 3 or way == piece]

    def y_hop(step):
        for s, way, piece in y_all:
            if s == step:
                y_wait(s, way, piece)
                if (s + 1, way, piece) in y_all:
                    y_send(s + 1, way, piece).start()

    def w_copy(d, m):
        src = (gate_w, up_w)[m].at[pl.ds(d * HALF, HALF)]
        return remote(src, wbuf.at[l * 2 + m], w_s.at[d, m], w_r.at[l * 2 + m], dev(x, yh * 2 + c, z, d))

    def w_local(m):
        src = (gate_w, up_w)[m].at[pl.ds(c * HALF, HALF)]
        return pltpu.make_async_copy(src, wbuf.at[l * 2 + m], w_r.at[l * 2 + m])

    def w_start():
        for m in range(2):
            for d in range(2):
                @pl.when(jnp.logical_or(c != l, c != d))
                def _():
                    w_copy(d, m).start()

            @pl.when(c == l)
            def _():
                w_local(m).start()

    def w_wait_recv():
        for j in range(4):
            pltpu.make_async_copy(wbuf.at[j], wbuf.at[j], w_r.at[j]).wait()

    def w_wait_send():
        for m in range(2):
            for d in range(2):
                @pl.when(jnp.logical_or(c != l, c != d))
                def _():
                    w_copy(d, m).wait_send()

    def near(h, b):
        return jnp.concatenate([tok[(y + d) % NY, b] for d in ORDER[h * 4 : h * 4 + 4]], axis=0)

    def select(h):
        r = lax.broadcasted_iota(jnp.int32, (NZ * RB, LANES), 0)
        q = lax.broadcasted_iota(jnp.int32, (NZ * RB, LANES), 1)
        wanted = jnp.where(q == (yh * NZ + r // RB) * 2 + l, 1.0, 0.0).astype(BF16)
        place = lax.dot_general(wanted, near(h, 0), (((1,), (1,)), ((), ())), preferred_element_type=F32)
        r = lax.broadcasted_iota(jnp.int32, place.shape, 0)
        q = lax.broadcasted_iota(jnp.int32, place.shape, 1)
        hit = jnp.logical_and(place == (r % 2 + 1).astype(F32), q // TOK == (r % RB) // 2)
        sel[...] = jnp.where(hit, 1.0, 0.0).astype(BF16)
        for b in range(0, BLK, 2):
            names = jnp.concatenate([near(h, 1 + b), near(h, 2 + b)], axis=1)
            got = jnp.dot(sel[...], names, preferred_element_type=F32).astype(BF16)
            zsend[h, :, :, b * LANES : (b + 2) * LANES] = got.reshape(NZ, RB, 2 * LANES)
        rows[x, 0, h] = zsend[h, z]

    def z_copy(h, j):
        d = ORDER[j]
        to = (z + NZ - d) % NZ
        return remote(zsend.at[h, to], rows.at[x, j, h], z_s.at[h, j], z_r.at[h, j], dev(x, y, to, c))

    def z_start(h):
        for j in range(1, NZ):
            z_copy(h, j).start()

    def x_refs(i, n, mine):
        j, h = PIECES[i]
        if n < 2:
            return rows.at[(x if mine else (xl, xr)[n]), j, h]
        at = (xl, xr)[n - 2] if mine else xo
        return rows.at[at, j, h, :, pl.ds((n - 2) * (HALF // 2), HALF // 2)]

    def x_copy(i, n):
        ref = x_refs(i, n, True)
        return remote(ref, ref, x_s.at[i, n], x_r.at[i, n], dev((xr, xl)[n % 2], y, z, c))

    def x_wait(i, n):
        ref = x_refs(i, n, False)
        remote(ref, ref, x_s.at[i, n], x_r.at[i, n], dev(xr, y, z, c)).wait_recv()

    def stage_b(i):
        j, h = PIECES[i]
        if j > 0:
            z_copy(h, j).wait_recv()
        x_copy(i, 0).start()
        x_copy(i, 1).start()

    def stage_c(i):
        for n in range(2):
            x_wait(i, n)
            x_copy(i, 2 + n).start()

    def stage_d(j):
        if j == 0:
            w_wait_recv()
        for h in range(NH):
            i = PIECES.index((j, h))
            x_wait(i, 2)
            x_wait(i, 3)
        for s in range(2):
            got = None
            for k in range(HALF // KC):
                cols = pl.ds(k * KC, KC)
                left = rows[:, j, :, :, cols].reshape(CR, KC)
                right = jnp.concatenate([wbuf[2 * s, cols], wbuf[2 * s + 1, cols]], axis=1)
                term = jnp.dot(left, right, preferred_element_type=F32)
                got = term if got is None else got + term
            acc[s, pl.ds(j * CR, CR)] = got

    def group_rows(g):
        first, last = GROUPS[g]
        return pl.ds(first * CR, (last - first) * CR)

    def p_copy(g):
        at = group_rows(g)
        return remote(acc.at[o, at], part.at[at], p_s.at[g], p_r.at[g], other_core)

    owner = dev(x, yh * 2 + c, z, l)

    def ho_remote(g):
        at = group_rows(g)
        return remote(hall.at[x, c, at], hown.at[at], ho_s.at[g], ho_r.at[g], owner)

    def ho_local(g):
        at = group_rows(g)
        return pltpu.make_async_copy(hall.at[x, c, at], hown.at[at], ho_r.at[g])

    def finish_hidden(g):
        p_copy(g).wait_recv()
        first, last = GROUPS[g]

        def body(j, carry):
            at = pl.ds(pl.multiple_of(j * CR, CR), CR)
            both = acc[c, at] + part[at]
            gate, up = both[:, :FB], both[:, FB:]
            hall[x, c, at] = (gate / (1.0 + jnp.exp(-gate)) * up).astype(BF16)
            return carry

        lax.fori_loop(first, last, body, 0)
        hx_copy(g, 0).start()
        hx_copy(g, 1).start()
        hc_copy(g, 0).start()

        @pl.when(c != l)
        def _():
            ho_remote(g).start()

        @pl.when(c == l)
        def _():
            ho_local(g).start()

    def hx_refs(g, n, mine):
        first, last = GROUPS[g]
        size = (last - first) * CR
        if n < 2:
            return hall.at[(x if mine else (xl, xr)[n]), c, pl.ds(first * CR, size)]
        at = (xl, xr)[n - 2] if mine else xo
        return hall.at[at, c, pl.ds(first * CR + (n - 2) * (size // 2), size // 2)]

    def hx_copy(g, n):
        ref = hx_refs(g, n, True)
        return remote(ref, ref, hx_s.at[g, n], hx_r.at[g, n], dev((xr, xl)[n % 2], y, z, c))

    def hx_wait(g, n):
        ref = hx_refs(g, n, False)
        remote(ref, ref, hx_s.at[g, n], hx_r.at[g, n], dev(xr, y, z, c)).wait_recv()

    def hc_copy(g, n):
        ref = hall.at[(x, xl, xr, xo)[n], c, group_rows(g)]
        return remote(ref, ref, hc_s.at[g, n], hc_r.at[g, n], other_core)

    def hc_wait(g, n):
        ref = hall.at[(x, xl, xr, xo)[n], o, group_rows(g)]
        remote(ref, ref, hc_s.at[g, n], hc_r.at[g, n], other_core).wait_recv()

    def relay_hidden(g):
        for n in range(2):
            hx_wait(g, n)
            hx_copy(g, 2 + n).start()
            hc_copy(g, 1 + n).start()

    def last_hidden(g):
        hx_wait(g, 2)
        hx_wait(g, 3)
        hc_copy(g, 3).start()

    def hess_cols(n):
        at = (x, xl, xr, xo)[n]
        return pl.ds(pl.multiple_of(at * 2 * FB, 2 * FB), 2 * FB)

    def hess_part(g, n):
        hc_wait(g, n)
        at = (x, xl, xr, xo)[n]
        r = group_rows(g)
        right = jnp.concatenate([hall[at, 0, r], hall[at, 1, r]], axis=1)
        got = lax.dot_general(hall[x, c, r], right, (((0,), (0,)), ((), ())), preferred_element_type=F32)
        cols = hess_cols(n)
        if g == 0:
            hess[:, cols] = got
        elif g < len(GROUPS) - 1:
            hess[:, cols] = hess[:, cols] + got
        else:
            hess[:, cols] = (hess[:, cols] + got) * scale_out

    def out_remote(n):
        cols = hess_cols(n)
        return remote(hess.at[:, cols], hess_out.at[:, cols], f_s.at[n], f_r.at[n], owner)

    def out_local(n):
        cols = hess_cols(n)
        return pltpu.make_async_copy(hess.at[:, cols], hess_out.at[:, cols], f_r.at[n])

    def out_start(n):
        @pl.when(c != l)
        def _():
            out_remote(n).start()

        @pl.when(c == l)
        def _():
            out_local(n).start()

    def restore():
        for g in range(len(GROUPS)):
            ho_local(g).wait()
        r = lax.broadcasted_iota(jnp.int32, (NZ * NH * RB, NZ * NH * RB), 0)
        q = lax.broadcasted_iota(jnp.int32, (NZ * NH * RB, NZ * NH * RB), 1)
        y_at = ((r // 32) % 4) * 2 + r // 128
        y_rank = rank_of((y_at + NY - (yh * 2 + c)) % NY)
        z_rank = rank_of(((r // 4) % NZ + NZ - z) % NZ)
        turn = jnp.where(q == z_rank * (NH * RB) + y_rank * 4 + r % 4, 1.0, 0.0).astype(BF16)
        for s in range(NX):
            block = jnp.concatenate([hown[j * CR + s * NH * RB : j * CR + (s + 1) * NH * RB] for j in range(NZ)], axis=0)
            hperm[s * 256 : (s + 1) * 256] = jnp.dot(turn, block, preferred_element_type=F32).astype(BF16)

    for piece in range(2):
        for way in range(2):
            y_send(0, way, piece).start()
    y_hop(0)
    y_hop(1)
    select(0)
    stage_b(0)
    z_start(0)
    y_hop(2)
    w_start()
    y_hop(3)
    select(1)
    z_start(1)
    stage_b(1)
    stage_c(0)
    stage_b(2)
    stage_b(3)
    stage_c(1)
    for i in range(4, 12):
        stage_b(i)
        stage_c(i - 2)
    stage_b(12)
    stage_c(10)
    stage_d(0)
    stage_d(1)
    stage_b(13)
    stage_c(11)
    stage_d(2)
    stage_b(14)
    stage_c(12)
    stage_d(3)
    p_copy(0).start()
    stage_b(15)
    stage_c(13)
    stage_d(4)
    finish_hidden(0)
    stage_c(14)
    stage_d(5)
    p_copy(1).start()
    stage_c(15)
    relay_hidden(0)
    finish_hidden(1)
    stage_d(6)
    stage_d(7)
    p_copy(2).start()
    last_hidden(0)
    relay_hidden(1)
    for n in range(4):
        hess_part(0, n)
    finish_hidden(2)
    last_hidden(1)
    for n in range(4):
        hess_part(1, n)
    hess_part(2, 0)
    out_start(0)
    relay_hidden(2)
    for n in (1, 2):
        hess_part(2, n)
        out_start(n)
    last_hidden(2)
    hess_part(2, 3)
    out_start(3)
    restore()
    hidden_copy = pltpu.make_async_copy(hperm, hidden_out, in_s.at[0])
    hidden_copy.start()

    for n in range(2):
        core_copy(n).wait_send()
    for step, way, piece in y_all:
        y_send(step, way, piece).wait_send()
    w_wait_send()
    for h in range(NH):
        for j in range(1, NZ):
            z_copy(h, j).wait_send()
    for i in range(len(PIECES)):
        for n in range(4):
            x_copy(i, n).wait_send()
    for g in range(len(GROUPS)):
        p_copy(g).wait_send()
        for n in range(4):
            hx_copy(g, n).wait_send()
            hc_copy(g, n).wait_send()

        @pl.when(c != l)
        def _():
            ho_remote(g).wait_send()

    for n in range(4):
        @pl.when(c != l)
        def _():
            out_remote(n).wait_send()

        out_local(n).wait()
    hidden_copy.wait()


def shards(codes, exponents, routes, gate_weight, up_weight):
    sem = pltpu.SemaphoreType.DMA
    hbm = pl.BlockSpec(memory_space=pl.ANY)
    scale_out = 1.0 / (TOK * NX * NY * NZ * 2 * routes.shape[1] // (NY * NZ))
    groups = len(GROUPS)
    hidden, hess = pl.pallas_call(
        functools.partial(kernel, scale_out),
        out_shape=(
            jax.ShapeDtypeStruct((SL, FB), BF16),
            jax.ShapeDtypeStruct((FB, NX * 2 * FB), F32),
        ),
        in_specs=[hbm] * 5,
        out_specs=(hbm, hbm),
        scratch_shapes=[
            pltpu.VMEM(codes.shape, BF16),
            pltpu.VMEM(exponents.shape, jnp.int32),
            pltpu.VMEM(routes.shape, jnp.int32),
            pltpu.VMEM((2 * BLK, TOK, LANES), F32),
            pltpu.VMEM((TOK, LANES), F32),
            pltpu.VMEM((BLK, TOK, LANES), F32),
            pltpu.VMEM((TOK, LANES), F32),
            pltpu.VMEM((NY, 1 + BLK, 2 * TOK, LANES), BF16),
            pltpu.VMEM((NZ * RB, 8 * TOK), BF16),
            pltpu.VMEM((NH, NZ, RB, HALF), BF16),
            pltpu.VMEM((NX, NZ, NH, RB, HALF), BF16),
            pltpu.VMEM((4, HALF, FB), BF16),
            pltpu.VMEM((2, SL, 2 * FB), F32),
            pltpu.VMEM((SL, 2 * FB), F32),
            pltpu.VMEM((NX, 2, SL, FB), BF16),
            pltpu.VMEM((SL, FB), BF16),
            pltpu.VMEM((SL, FB), BF16),
            pltpu.VMEM((FB, NX * 2 * FB), F32),
            sem((3,)),
            sem((2,)),
            sem((2,)),
            sem((4, 2, 2)),
            sem((4, 2, 2)),
            sem((NH, NZ)),
            sem((NH, NZ)),
            sem((len(PIECES), 4)),
            sem((len(PIECES), 4)),
            sem((2, 2)),
            sem((4,)),
            sem((groups,)),
            sem((groups,)),
            sem((groups, 4)),
            sem((groups, 4)),
            sem((groups, 4)),
            sem((groups, 4)),
            sem((groups,)),
            sem((groups,)),
            sem((4,)),
            sem((4,)),
        ],
        compiler_params=pltpu.CompilerParams(
            collective_id=0, has_side_effects=True, vmem_limit_bytes=60 * 1024 * 1024
        ),
        name="routed_stats",
    )(codes, exponents, routes, gate_weight[0], up_weight[0])
    return hidden[None], hess[None]


def solution(mesh):
    placed = (
        P(("dp", "expert"), None),
        P(("dp", "expert"), None),
        P(("dp", "expert"), None),
        P("expert", None, "dp"),
        P("expert", None, "dp"),
    )
    return jax.shard_map(
        shards,
        mesh=mesh,
        in_specs=placed,
        out_specs=(P("expert", None, "dp"), P("expert", "dp", None)),
        check_vma=False,
    )
```

```python
import functools

import jax
import jax.numpy as jnp
from jax import lax
from jax.experimental import pallas as pl
from jax.experimental.pallas import tpu as pltpu
from jax.sharding import PartitionSpec as P

MESH = pl.DeviceIdType.MESH
F32 = jnp.float32
BF16 = jnp.bfloat16

NX, NY, NZ = 4, 8, 8
TOK = 8
D = 7168
HALF = D // 2
LANES = 128
BLK = HALF // LANES
CUT = 15
NH = 2
RB = 16
CR = NX * NH * RB
SL = NZ * CR
FB = 128
KC = 512
ORDER = (0, 1, 7, 2, 6, 3, 5, 4)
GROUPS = ((0, 4), (4, 8))
PIECES = [(0, 0), (1, 0), (2, 0), (0, 1), (1, 1), (2, 1), (3, 0), (4, 0), (3, 1), (4, 1)]
PIECES += [(5, 0), (6, 0), (5, 1), (6, 1), (7, 0), (7, 1)]
AHEAD = 4
PLAN = (
    "B3", "C1", "B4", "C2", "B5", "C3", "B6", "C4", "B7", "C5", "B8", "C6", "B9", "C7", "B10", "C8",
    "B11", "C9", "B12", "C10", "B13", "C11", "B14", "C12", "B15", "D0", "D1", "C13", "D2", "D3", "P0", "C14",
    "D4", "C15", "F0", "D5", "D6", "D7", "P1", "R0", "F1", "L0", "R1", "H0", "E0", "E1", "E2", "L1",
    "E3",
)


def rank_of(distance):
    rank = jnp.zeros_like(distance)
    for j, d in enumerate(ORDER):
        rank = jnp.where(distance == d, j, rank)
    return rank


def kernel(
    scale_out,
    codes_in,
    exponents_in,
    routes_in,
    gate_w,
    up_w,
    hidden_out,
    hess_out,
    codes,
    exponents,
    routes,
    deq,
    table,
    deq_in,
    table_in,
    tok,
    sel,
    zsend,
    rows,
    wbuf,
    acc,
    part,
    hall,
    hown,
    hperm,
    hess,
    in_s,
    core_s,
    core_r,
    y_s,
    y_r,
    z_s,
    z_r,
    x_s,
    x_r,
    w_s,
    w_r,
    p_s,
    p_r,
    hx_s,
    hx_r,
    hc_s,
    hc_r,
    ho_s,
    ho_r,
    f_s,
    f_r,
):
    dp = lax.axis_index("dp")
    ex = lax.axis_index("expert")
    x, l = dp // 2, dp % 2
    yh, z, c = ex // (2 * NZ), (ex // 2) % NZ, ex % 2
    y = yh * 2 + l
    o = 1 - c
    xr, xl, xo = (x + 1) % NX, (x + 3) % NX, (x + 2) % NX
    yr, yl = (y + 1) % NY, (y + NY - 1) % NY

    def dev(dx, dy, dz, dc):
        return (dx * 2 + dy % 2, ((dy // 2) * NZ + dz) * 2 + dc)

    def remote(src, dst, send, recv, to):
        return pltpu.make_async_remote_copy(
            src_ref=src, dst_ref=dst, send_sem=send, recv_sem=recv, device_id=to, device_id_type=MESH
        )

    def ring(n, act):
        def body(j, carry):
            act(j)
            return carry

        lax.fori_loop(1, n, body, 0)

    other_core = dev(x, y, z, o)
    y_pair = yh * 2 + (1 - l)

    inputs = [
        pltpu.make_async_copy(routes_in, routes, in_s.at[0]),
        pltpu.make_async_copy(exponents_in, exponents, in_s.at[1]),
        pltpu.make_async_copy(codes_in, codes, in_s.at[2]),
    ]
    for copy in inputs:
        copy.start()

    barrier = pltpu.get_barrier_semaphore()

    def greet(to):
        pl.semaphore_signal(barrier, inc=1, device_id=to, device_id_type=MESH)

    greet(other_core)
    greet(dev(x, y_pair, z, o))
    greet(dev(x, yr, z, c))
    greet(dev(x, yl, z, c))
    greet(dev(xr, y, z, c))
    greet(dev(xl, y, z, c))
    ring(NZ, lambda j: greet(dev(x, y, (z + j) % NZ, c)))

    inputs[0].wait()
    rv = routes[...]
    lane = lax.broadcasted_iota(jnp.int32, (TOK, LANES), 1)
    chosen = jnp.zeros((TOK, LANES), F32)
    for t in range(rv.shape[1]):
        chosen = jnp.where(rv[:, t : t + 1] == lane, 1.0, chosen)
    row = lax.broadcasted_iota(jnp.int32, (TOK, LANES), 0)
    order = chosen
    for t in range(TOK - 1):
        order = order + jnp.where(row > t, chosen[t : t + 1, :], 0.0)
    table[...] = chosen * order
    inputs[1].wait()
    inputs[2].wait()
    ev = exponents[...]
    scale = jnp.zeros(ev.shape, F32)
    for e in range(-2, 2):
        scale = jnp.where(ev == e, jnp.float32(2.0**e), scale)
    for b in range(2 * BLK):
        deq[b] = codes[:, b * LANES : (b + 1) * LANES].astype(F32) * scale[:, b : b + 1]

    pl.semaphore_wait(barrier, 13)

    def core_copy(n):
        if n == 0:
            return remote(deq.at[pl.ds(o * BLK, BLK)], deq_in, core_s.at[0], core_r.at[0], other_core)
        return remote(table, table_in, core_s.at[1], core_r.at[1], other_core)

    for n in range(2):
        core_copy(n).start()
    for n in range(2):
        core_copy(n).wait_recv()

    def pack(own, oth):
        return jnp.concatenate([jnp.where(c == 0, own, oth), jnp.where(c == 0, oth, own)], axis=0).astype(BF16)

    tok[y, 0] = pack(table[...], table_in[...])

    def assemble(j, carry):
        tok[y, 1 + j] = pack(deq[c * BLK + j], deq_in[j])
        return carry

    lax.fori_loop(0, BLK, assemble, 0, unroll=4)

    def y_ref(src_y, piece):
        return tok.at[src_y, pl.ds(0, CUT) if piece == 0 else pl.ds(CUT, 1 + BLK - CUT)]

    def y_send(step, way, piece):
        src = (y + NY - step) % NY if way == 0 else (y + step) % NY
        to = yr if way == 0 else yl
        ref = y_ref(src, piece)
        return remote(ref, ref, y_s.at[step, way, piece], y_r.at[step, way, piece], dev(x, to, z, c))

    def y_wait(step, way, piece):
        src = (y + NY - step - 1) % NY if way == 0 else (y + step + 1) % NY
        ref = y_ref(src, piece)
        remote(ref, ref, y_s.at[step, way, piece], y_r.at[step, way, piece], dev(x, yr, z, c)).wait_recv()

    y_all = [(step, way, piece) for step in range(4) for piece in range(2) for way in range(2) if step < 3 or way == piece]

    def y_hop(step):
        for s, way, piece in y_all:
            if s == step:
                y_wait(s, way, piece)
                if (s + 1, way, piece) in y_all:
                    y_send(s + 1, way, piece).start()

    def w_copy(d, m):
        src = (gate_w, up_w)[m].at[pl.ds(d * HALF, HALF)]
        return remote(src, wbuf.at[l * 2 + m], w_s.at[d, m], w_r.at[l * 2 + m], dev(x, yh * 2 + c, z, d))

    def w_local(m):
        src = (gate_w, up_w)[m].at[pl.ds(c * HALF, HALF)]
        return pltpu.make_async_copy(src, wbuf.at[l * 2 + m], w_r.at[l * 2 + m])

    def w_start():
        for m in range(2):
            for d in range(2):
                @pl.when(jnp.logical_or(c != l, c != d))
                def _():
                    w_copy(d, m).start()

            @pl.when(c == l)
            def _():
                w_local(m).start()

    def w_wait_recv():
        for j in range(4):
            pltpu.make_async_copy(wbuf.at[j], wbuf.at[j], w_r.at[j]).wait()

    def w_wait_send():
        for m in range(2):
            for d in range(2):
                @pl.when(jnp.logical_or(c != l, c != d))
                def _():
                    w_copy(d, m).wait_send()

    def near(h, b):
        return jnp.concatenate([tok[(y + d) % NY, b] for d in ORDER[h * 4 : h * 4 + 4]], axis=0)

    def select(h):
        r = lax.broadcasted_iota(jnp.int32, (NZ * RB, LANES), 0)
        q = lax.broadcasted_iota(jnp.int32, (NZ * RB, LANES), 1)
        wanted = jnp.where(q == (yh * NZ + r // RB) * 2 + l, 1.0, 0.0).astype(BF16)
        place = lax.dot_general(wanted, near(h, 0), (((1,), (1,)), ((), ())), preferred_element_type=F32)
        r = lax.broadcasted_iota(jnp.int32, place.shape, 0)
        q = lax.broadcasted_iota(jnp.int32, place.shape, 1)
        hit = jnp.logical_and(place == (r % 2 + 1).astype(F32), q // TOK == (r % RB) // 2)
        sel[...] = jnp.where(hit, 1.0, 0.0).astype(BF16)
        for b in range(0, BLK, 2):
            names = jnp.concatenate([near(h, 1 + b), near(h, 2 + b)], axis=1)
            got = jnp.dot(sel[...], names, preferred_element_type=F32).astype(BF16)
            zsend[h, :, :, b * LANES : (b + 2) * LANES] = got.reshape(NZ, RB, 2 * LANES)
        rows[x, 0, h] = zsend[h, z]

    def z_copy(h, j):
        d = ORDER[j]
        to = (z + NZ - d) % NZ
        return remote(zsend.at[h, to], rows.at[x, j, h], z_s.at[h, j], z_r.at[h, j], dev(x, y, to, c))

    z_order = [(h, j) for j, h in PIECES if j > 0]

    def z_start(n):
        if n < len(z_order):
            z_copy(*z_order[n]).start()

    def x_refs(i, n, mine):
        j, h = PIECES[i]
        if n < 2:
            return rows.at[(x if mine else (xl, xr)[n]), j, h]
        at = (xl, xr)[n - 2] if mine else xo
        return rows.at[at, j, h, :, pl.ds((n - 2) * (HALF // 2), HALF // 2)]

    def x_copy(i, n):
        ref = x_refs(i, n, True)
        return remote(ref, ref, x_s.at[i, n], x_r.at[i, n], dev((xr, xl)[n % 2], y, z, c))

    def x_wait(i, n):
        ref = x_refs(i, n, False)
        remote(ref, ref, x_s.at[i, n], x_r.at[i, n], dev(xr, y, z, c)).wait_recv()

    def stage_b(i):
        j, h = PIECES[i]
        if j > 0:
            z_copy(h, j).wait_recv()
            z_start(z_order.index((h, j)) + AHEAD)
        x_copy(i, 0).start()
        x_copy(i, 1).start()

    def stage_c(i):
        for n in range(2):
            x_wait(i, n)
            x_copy(i, 2 + n).start()

    def stage_d(j):
        if j == 0:
            w_wait_recv()
        for h in range(NH):
            i = PIECES.index((j, h))
            x_wait(i, 2)
            x_wait(i, 3)
        for s in range(2):
            got = None
            for k in range(HALF // KC):
                cols = pl.ds(k * KC, KC)
                left = rows[:, j, :, :, cols].reshape(CR, KC)
                right = jnp.concatenate([wbuf[2 * s, cols], wbuf[2 * s + 1, cols]], axis=1)
                term = jnp.dot(left, right, preferred_element_type=F32)
                got = term if got is None else got + term
            acc[s, pl.ds(j * CR, CR)] = got

    def group_rows(g):
        first, last = GROUPS[g]
        return pl.ds(first * CR, (last - first) * CR)

    def p_copy(g):
        at = group_rows(g)
        return remote(acc.at[o, at], part.at[at], p_s.at[g], p_r.at[g], other_core)

    owner = dev(x, yh * 2 + c, z, l)

    def ho_remote(g):
        at = group_rows(g)
        return remote(hall.at[x, c, at], hown.at[at], ho_s.at[g], ho_r.at[g], owner)

    def ho_local(g):
        at = group_rows(g)
        return pltpu.make_async_copy(hall.at[x, c, at], hown.at[at], ho_r.at[g])

    def finish_hidden(g):
        p_copy(g).wait_recv()
        first, last = GROUPS[g]

        def body(j, carry):
            at = pl.ds(pl.multiple_of(j * CR, CR), CR)
            both = acc[c, at] + part[at]
            gate, up = both[:, :FB], both[:, FB:]
            hall[x, c, at] = (gate / (1.0 + jnp.exp(-gate)) * up).astype(BF16)
            return carry

        lax.fori_loop(first, last, body, 0)
        hx_copy(g, 0).start()
        hx_copy(g, 1).start()
        hc_copy(g, 0).start()

        @pl.when(c != l)
        def _():
            ho_remote(g).start()

        @pl.when(c == l)
        def _():
            ho_local(g).start()

    def hx_refs(g, n, mine):
        first, last = GROUPS[g]
        size = (last - first) * CR
        if n < 2:
            return hall.at[(x if mine else (xl, xr)[n]), c, pl.ds(first * CR, size)]
        at = (xl, xr)[n - 2] if mine else xo
        return hall.at[at, c, pl.ds(first * CR + (n - 2) * (size // 2), size // 2)]

    def hx_copy(g, n):
        ref = hx_refs(g, n, True)
        return remote(ref, ref, hx_s.at[g, n], hx_r.at[g, n], dev((xr, xl)[n % 2], y, z, c))

    def hx_wait(g, n):
        ref = hx_refs(g, n, False)
        remote(ref, ref, hx_s.at[g, n], hx_r.at[g, n], dev(xr, y, z, c)).wait_recv()

    def hc_copy(g, n):
        ref = hall.at[(x, xl, xr, xo)[n], c, group_rows(g)]
        return remote(ref, ref, hc_s.at[g, n], hc_r.at[g, n], other_core)

    def hc_wait(g, n):
        ref = hall.at[(x, xl, xr, xo)[n], o, group_rows(g)]
        remote(ref, ref, hc_s.at[g, n], hc_r.at[g, n], other_core).wait_recv()

    def relay_hidden(g):
        for n in range(2):
            hx_wait(g, n)
            hx_copy(g, 2 + n).start()
            hc_copy(g, 1 + n).start()

    def last_hidden(g):
        hx_wait(g, 2)
        hx_wait(g, 3)
        hc_copy(g, 3).start()

    def hess_cols(n):
        at = (x, xl, xr, xo)[n]
        return pl.ds(pl.multiple_of(at * 2 * FB, 2 * FB), 2 * FB)

    def hess_part(g, n):
        hc_wait(g, n)
        at = (x, xl, xr, xo)[n]
        r = group_rows(g)
        right = jnp.concatenate([hall[at, 0, r], hall[at, 1, r]], axis=1)
        got = lax.dot_general(hall[x, c, r], right, (((0,), (0,)), ((), ())), preferred_element_type=F32)
        cols = hess_cols(n)
        if g > 0:
            got = hess[:, cols] + got
        hess[:, cols] = got * scale_out if g == len(GROUPS) - 1 else got

    def out_remote(n):
        cols = hess_cols(n)
        return remote(hess.at[:, cols], hess_out.at[:, cols], f_s.at[n], f_r.at[n], owner)

    def out_local(n):
        cols = hess_cols(n)
        return pltpu.make_async_copy(hess.at[:, cols], hess_out.at[:, cols], f_r.at[n])

    def out_start(n):
        @pl.when(c != l)
        def _():
            out_remote(n).start()

        @pl.when(c == l)
        def _():
            out_local(n).start()

    def restore():
        for g in range(len(GROUPS)):
            ho_local(g).wait()
        r = lax.broadcasted_iota(jnp.int32, (NZ * NH * RB, NZ * NH * RB), 0)
        q = lax.broadcasted_iota(jnp.int32, (NZ * NH * RB, NZ * NH * RB), 1)
        y_at = ((r // 32) % 4) * 2 + r // 128
        y_rank = rank_of((y_at + NY - (yh * 2 + c)) % NY)
        z_rank = rank_of(((r // 4) % NZ + NZ - z) % NZ)
        turn = jnp.where(q == z_rank * (NH * RB) + y_rank * 4 + r % 4, 1.0, 0.0).astype(BF16)
        for s in range(NX):
            block = jnp.concatenate([hown[j * CR + s * NH * RB : j * CR + (s + 1) * NH * RB] for j in range(NZ)], axis=0)
            hperm[s * 256 : (s + 1) * 256] = jnp.dot(turn, block, preferred_element_type=F32).astype(BF16)

    for piece in range(2):
        for way in range(2):
            y_send(0, way, piece).start()
    y_hop(0)
    y_hop(1)
    select(0)
    stage_b(0)
    z_start(0)
    z_start(1)
    y_hop(2)
    w_start()
    stage_b(1)
    stage_c(0)
    y_hop(3)
    select(1)
    for n in range(2, AHEAD):
        z_start(n)
    stage_b(2)
    acts = {"B": stage_b, "C": stage_c, "D": stage_d, "F": finish_hidden, "R": relay_hidden, "L": last_hidden}
    for step in PLAN:
        act, n = step[0], int(step[1:])
        if act == "P":
            p_copy(n).start()
        elif act == "H":
            for m in range(4):
                hess_part(n, m)
        elif act == "E":
            hess_part(len(GROUPS) - 1, n)
            out_start(n)
        else:
            acts[act](n)
    restore()
    hidden_copy = pltpu.make_async_copy(hperm, hidden_out, in_s.at[0])
    hidden_copy.start()

    for n in range(2):
        core_copy(n).wait_send()
    for step, way, piece in y_all:
        y_send(step, way, piece).wait_send()
    w_wait_send()
    for h in range(NH):
        for j in range(1, NZ):
            z_copy(h, j).wait_send()
    for i in range(len(PIECES)):
        for n in range(4):
            x_copy(i, n).wait_send()
    for g in range(len(GROUPS)):
        p_copy(g).wait_send()
        for n in range(4):
            hx_copy(g, n).wait_send()
            hc_copy(g, n).wait_send()

        @pl.when(c != l)
        def _():
            ho_remote(g).wait_send()

    for n in range(4):
        @pl.when(c != l)
        def _():
            out_remote(n).wait_send()

        out_local(n).wait()
    hidden_copy.wait()


def shards(codes, exponents, routes, gate_weight, up_weight):
    sem = pltpu.SemaphoreType.DMA
    hbm = pl.BlockSpec(memory_space=pl.ANY)
    scale_out = 1.0 / (TOK * NX * NY * NZ * 2 * routes.shape[1] // (NY * NZ))
    groups = len(GROUPS)
    hidden, hess = pl.pallas_call(
        functools.partial(kernel, scale_out),
        out_shape=(
            jax.ShapeDtypeStruct((SL, FB), BF16),
            jax.ShapeDtypeStruct((FB, NX * 2 * FB), F32),
        ),
        in_specs=[hbm] * 5,
        out_specs=(hbm, hbm),
        scratch_shapes=[
            pltpu.VMEM(codes.shape, BF16),
            pltpu.VMEM(exponents.shape, jnp.int32),
            pltpu.VMEM(routes.shape, jnp.int32),
            pltpu.VMEM((2 * BLK, TOK, LANES), F32),
            pltpu.VMEM((TOK, LANES), F32),
            pltpu.VMEM((BLK, TOK, LANES), F32),
            pltpu.VMEM((TOK, LANES), F32),
            pltpu.VMEM((NY, 1 + BLK, 2 * TOK, LANES), BF16),
            pltpu.VMEM((NZ * RB, 8 * TOK), BF16),
            pltpu.VMEM((NH, NZ, RB, HALF), BF16),
            pltpu.VMEM((NX, NZ, NH, RB, HALF), BF16),
            pltpu.VMEM((4, HALF, FB), BF16),
            pltpu.VMEM((2, SL, 2 * FB), F32),
            pltpu.VMEM((SL, 2 * FB), F32),
            pltpu.VMEM((NX, 2, SL, FB), BF16),
            pltpu.VMEM((SL, FB), BF16),
            pltpu.VMEM((SL, FB), BF16),
            pltpu.VMEM((FB, NX * 2 * FB), F32),
            sem((3,)),
            sem((2,)),
            sem((2,)),
            sem((4, 2, 2)),
            sem((4, 2, 2)),
            sem((NH, NZ)),
            sem((NH, NZ)),
            sem((len(PIECES), 4)),
            sem((len(PIECES), 4)),
            sem((2, 2)),
            sem((4,)),
            sem((groups,)),
            sem((groups,)),
            sem((groups, 4)),
            sem((groups, 4)),
            sem((groups, 4)),
            sem((groups, 4)),
            sem((groups,)),
            sem((groups,)),
            sem((4,)),
            sem((4,)),
        ],
        compiler_params=pltpu.CompilerParams(
            collective_id=0, has_side_effects=True, vmem_limit_bytes=60 * 1024 * 1024
        ),
        name="routed_stats",
    )(codes, exponents, routes, gate_weight[0], up_weight[0])
    return hidden[None], hess[None]


def solution(mesh):
    placed = (
        P(("dp", "expert"), None),
        P(("dp", "expert"), None),
        P(("dp", "expert"), None),
        P("expert", None, "dp"),
        P("expert", None, "dp"),
    )
    return jax.shard_map(
        shards,
        mesh=mesh,
        in_specs=placed,
        out_specs=(P("expert", None, "dp"), P("expert", "dp", None)),
        check_vma=False,
    )
```

```python
import functools

import jax
import jax.numpy as jnp
from jax import lax
from jax.experimental import pallas as pl
from jax.experimental.pallas import tpu as pltpu
from jax.sharding import PartitionSpec as P

MESH = pl.DeviceIdType.MESH
F32 = jnp.float32
BF16 = jnp.bfloat16

NX, NY, NZ = 4, 8, 8
TOK = 8
D = 7168
HALF = D // 2
LANES = 128
BLK = HALF // LANES
CUT = 15
NH = 2
RB = 16
CR = NX * NH * RB
SL = NZ * CR
FB = 128
KC = 512
ORDER = (0, 1, 7, 2, 6, 3, 5, 4)
GROUPS = ((0, 4), (4, 8))
PIECES = [(0, 0), (1, 0), (2, 0), (0, 1), (1, 1), (2, 1), (3, 0), (4, 0), (3, 1), (4, 1)]
PIECES += [(5, 0), (6, 0), (5, 1), (6, 1), (7, 0), (7, 1)]
AHEAD = 4
PLAN = (
    "B3", "C1", "B4", "C2", "B5", "C3", "B6", "C4", "B7", "C5", "B8", "C6", "B9", "C7", "B10", "C8",
    "B11", "C9", "B12", "C10", "B13", "C11", "B14", "C12", "B15", "C13", "D0", "D1", "C14", "D2", "D3", "C15",
    "D4", "F0", "D5", "D6", "D7", "R0", "F1", "L0", "R1", "H0", "E0", "E1", "E2", "L1", "E3",
)


def rank_of(distance):
    rank = jnp.zeros_like(distance)
    for j, d in enumerate(ORDER):
        rank = jnp.where(distance == d, j, rank)
    return rank


def kernel(
    scale_out,
    codes_in,
    exponents_in,
    routes_in,
    gate_w,
    up_w,
    hidden_out,
    hess_out,
    codes,
    exponents,
    routes,
    deq,
    table,
    deq_in,
    table_in,
    tok,
    sel,
    zsend,
    rows,
    wbuf,
    acc,
    part,
    hall,
    hown,
    hperm,
    hess,
    in_s,
    core_s,
    core_r,
    y_s,
    y_r,
    z_s,
    z_r,
    x_s,
    x_r,
    w_s,
    w_r,
    p_s,
    p_r,
    hx_s,
    hx_r,
    hc_s,
    hc_r,
    ho_s,
    ho_r,
    f_s,
    f_r,
):
    dp = lax.axis_index("dp")
    ex = lax.axis_index("expert")
    x, l = dp // 2, dp % 2
    yh, z, c = ex // (2 * NZ), (ex // 2) % NZ, ex % 2
    y = yh * 2 + l
    o = 1 - c
    xr, xl, xo = (x + 1) % NX, (x + 3) % NX, (x + 2) % NX
    yr, yl = (y + 1) % NY, (y + NY - 1) % NY

    def dev(dx, dy, dz, dc):
        return (dx * 2 + dy % 2, ((dy // 2) * NZ + dz) * 2 + dc)

    def remote(src, dst, send, recv, to):
        return pltpu.make_async_remote_copy(
            src_ref=src, dst_ref=dst, send_sem=send, recv_sem=recv, device_id=to, device_id_type=MESH
        )

    def ring(n, act):
        def body(j, carry):
            act(j)
            return carry

        lax.fori_loop(1, n, body, 0)

    other_core = dev(x, y, z, o)
    y_pair = yh * 2 + (1 - l)

    inputs = [
        pltpu.make_async_copy(routes_in, routes, in_s.at[0]),
        pltpu.make_async_copy(exponents_in, exponents, in_s.at[1]),
        pltpu.make_async_copy(codes_in, codes, in_s.at[2]),
    ]
    for copy in inputs:
        copy.start()

    barrier = pltpu.get_barrier_semaphore()

    def greet(to):
        pl.semaphore_signal(barrier, inc=1, device_id=to, device_id_type=MESH)

    greet(other_core)
    greet(dev(x, y_pair, z, o))
    greet(dev(x, yr, z, c))
    greet(dev(x, yl, z, c))
    greet(dev(xr, y, z, c))
    greet(dev(xl, y, z, c))
    ring(NZ, lambda j: greet(dev(x, y, (z + j) % NZ, c)))

    inputs[0].wait()
    rv = routes[...]
    lane = lax.broadcasted_iota(jnp.int32, (TOK, LANES), 1)
    chosen = jnp.zeros((TOK, LANES), F32)
    for t in range(rv.shape[1]):
        chosen = jnp.where(rv[:, t : t + 1] == lane, 1.0, chosen)
    row = lax.broadcasted_iota(jnp.int32, (TOK, LANES), 0)
    order = chosen
    for t in range(TOK - 1):
        order = order + jnp.where(row > t, chosen[t : t + 1, :], 0.0)
    table[...] = chosen * order
    inputs[1].wait()
    inputs[2].wait()
    ev = exponents[...]
    scale = jnp.zeros(ev.shape, F32)
    for e in range(-2, 2):
        scale = jnp.where(ev == e, jnp.float32(2.0**e), scale)
    for b in range(2 * BLK):
        deq[b] = codes[:, b * LANES : (b + 1) * LANES].astype(F32) * scale[:, b : b + 1]

    pl.semaphore_wait(barrier, 13)

    def core_copy(n):
        if n == 0:
            return remote(deq.at[pl.ds(o * BLK, BLK)], deq_in, core_s.at[0], core_r.at[0], other_core)
        return remote(table, table_in, core_s.at[1], core_r.at[1], other_core)

    for n in range(2):
        core_copy(n).start()
    for n in range(2):
        core_copy(n).wait_recv()

    def pack(own, oth):
        return jnp.concatenate([jnp.where(c == 0, own, oth), jnp.where(c == 0, oth, own)], axis=0).astype(BF16)

    tok[y, 0] = pack(table[...], table_in[...])

    def assemble(j, carry):
        tok[y, 1 + j] = pack(deq[c * BLK + j], deq_in[j])
        return carry

    lax.fori_loop(0, BLK, assemble, 0, unroll=4)

    def y_ref(src_y, piece):
        return tok.at[src_y, pl.ds(0, CUT) if piece == 0 else pl.ds(CUT, 1 + BLK - CUT)]

    def y_send(step, way, piece):
        src = (y + NY - step) % NY if way == 0 else (y + step) % NY
        to = yr if way == 0 else yl
        ref = y_ref(src, piece)
        return remote(ref, ref, y_s.at[step, way, piece], y_r.at[step, way, piece], dev(x, to, z, c))

    def y_wait(step, way, piece):
        src = (y + NY - step - 1) % NY if way == 0 else (y + step + 1) % NY
        ref = y_ref(src, piece)
        remote(ref, ref, y_s.at[step, way, piece], y_r.at[step, way, piece], dev(x, yr, z, c)).wait_recv()

    y_all = [(step, way, piece) for step in range(4) for piece in range(2) for way in range(2) if step < 3 or way == piece]

    def y_hop(step):
        for s, way, piece in y_all:
            if s == step:
                y_wait(s, way, piece)
                if (s + 1, way, piece) in y_all:
                    y_send(s + 1, way, piece).start()

    def w_copy(d, m):
        src = (gate_w, up_w)[m].at[pl.ds(d * HALF, HALF)]
        return remote(src, wbuf.at[l * 2 + m], w_s.at[d, m], w_r.at[l * 2 + m], dev(x, yh * 2 + c, z, d))

    def w_local(m):
        src = (gate_w, up_w)[m].at[pl.ds(c * HALF, HALF)]
        return pltpu.make_async_copy(src, wbuf.at[l * 2 + m], w_r.at[l * 2 + m])

    def w_start():
        for m in range(2):
            for d in range(2):
                @pl.when(jnp.logical_or(c != l, c != d))
                def _():
                    w_copy(d, m).start()

            @pl.when(c == l)
            def _():
                w_local(m).start()

    def w_wait_recv():
        for j in range(4):
            pltpu.make_async_copy(wbuf.at[j], wbuf.at[j], w_r.at[j]).wait()

    def w_wait_send():
        for m in range(2):
            for d in range(2):
                @pl.when(jnp.logical_or(c != l, c != d))
                def _():
                    w_copy(d, m).wait_send()

    def near(h, b):
        return jnp.concatenate([tok[(y + d) % NY, b] for d in ORDER[h * 4 : h * 4 + 4]], axis=0)

    def select(h):
        r = lax.broadcasted_iota(jnp.int32, (NZ * RB, LANES), 0)
        q = lax.broadcasted_iota(jnp.int32, (NZ * RB, LANES), 1)
        wanted = jnp.where(q == (yh * NZ + r // RB) * 2 + l, 1.0, 0.0).astype(BF16)
        place = lax.dot_general(wanted, near(h, 0), (((1,), (1,)), ((), ())), preferred_element_type=F32)
        r = lax.broadcasted_iota(jnp.int32, place.shape, 0)
        q = lax.broadcasted_iota(jnp.int32, place.shape, 1)
        hit = jnp.logical_and(place == (r % 2 + 1).astype(F32), q // TOK == (r % RB) // 2)
        sel[...] = jnp.where(hit, 1.0, 0.0).astype(BF16)

    def fill(h, first, last):
        to = [(z + NZ - d) % NZ for d in ORDER[first:last]]
        chosen = jnp.concatenate([sel[pl.ds(pl.multiple_of(t * RB, RB), RB)] for t in to], axis=0)
        for b in range(0, BLK, 2):
            names = jnp.concatenate([near(h, 1 + b), near(h, 2 + b)], axis=1)
            got = jnp.dot(chosen, names, preferred_element_type=F32).astype(BF16)
            for n, t in enumerate(to):
                piece = got[n * RB : (n + 1) * RB]
                if first + n == 0:
                    rows[x, 0, h, :, b * LANES : (b + 2) * LANES] = piece
                else:
                    zsend[h, t, :, b * LANES : (b + 2) * LANES] = piece

    def z_copy(h, j):
        d = ORDER[j]
        to = (z + NZ - d) % NZ
        return remote(zsend.at[h, to], rows.at[x, j, h], z_s.at[h, j], z_r.at[h, j], dev(x, y, to, c))

    z_order = [(h, j) for j, h in PIECES if j > 0]

    def z_start(n):
        if n < len(z_order):
            z_copy(*z_order[n]).start()

    def x_refs(i, n, mine):
        j, h = PIECES[i]
        if n < 2:
            return rows.at[(x if mine else (xl, xr)[n]), j, h]
        at = (xl, xr)[n - 2] if mine else xo
        return rows.at[at, j, h, :, pl.ds((n - 2) * (HALF // 2), HALF // 2)]

    def x_copy(i, n):
        ref = x_refs(i, n, True)
        return remote(ref, ref, x_s.at[i, n], x_r.at[i, n], dev((xr, xl)[n % 2], y, z, c))

    def x_wait(i, n):
        ref = x_refs(i, n, False)
        remote(ref, ref, x_s.at[i, n], x_r.at[i, n], dev(xr, y, z, c)).wait_recv()

    def stage_b(i):
        j, h = PIECES[i]
        if j > 0:
            z_copy(h, j).wait_recv()
            z_start(z_order.index((h, j)) + AHEAD)
        x_copy(i, 0).start()
        x_copy(i, 1).start()

    def stage_c(i):
        for n in range(2):
            x_wait(i, n)
            x_copy(i, 2 + n).start()

    def stage_d(j):
        if j == 0:
            w_wait_recv()
        for h in range(NH):
            i = PIECES.index((j, h))
            x_wait(i, 2)
            x_wait(i, 3)
        for s in range(2):
            got = None
            for k in range(HALF // KC):
                cols = pl.ds(k * KC, KC)
                left = rows[:, j, :, :, cols].reshape(CR, KC)
                right = jnp.concatenate([wbuf[2 * s, cols], wbuf[2 * s + 1, cols]], axis=1)
                term = jnp.dot(left, right, preferred_element_type=F32)
                got = term if got is None else got + term
            acc[s, pl.ds(j * CR, CR)] = got
        p_copy(j).start()

    def group_rows(g):
        first, last = GROUPS[g]
        return pl.ds(first * CR, (last - first) * CR)

    def p_copy(j):
        at = pl.ds(j * CR, CR)
        return remote(acc.at[o, at], part.at[at], p_s.at[j], p_r.at[j], other_core)

    owner = dev(x, yh * 2 + c, z, l)

    def ho_remote(g):
        at = group_rows(g)
        return remote(hall.at[x, c, at], hown.at[at], ho_s.at[g], ho_r.at[g], owner)

    def ho_local(g):
        at = group_rows(g)
        return pltpu.make_async_copy(hall.at[x, c, at], hown.at[at], ho_r.at[g])

    def finish_hidden(g):
        for j in range(*GROUPS[g]):
            p_copy(j).wait_recv()
            at = pl.ds(j * CR, CR)
            both = acc[c, at] + part[at]
            gate, up = both[:, :FB], both[:, FB:]
            hall[x, c, at] = (gate / (1.0 + jnp.exp(-gate)) * up).astype(BF16)
        hx_copy(g, 0).start()
        hx_copy(g, 1).start()
        hc_copy(g, 0).start()

        @pl.when(c != l)
        def _():
            ho_remote(g).start()

        @pl.when(c == l)
        def _():
            ho_local(g).start()

    def hx_refs(g, n, mine):
        first, last = GROUPS[g]
        size = (last - first) * CR
        if n < 2:
            return hall.at[(x if mine else (xl, xr)[n]), c, pl.ds(first * CR, size)]
        at = (xl, xr)[n - 2] if mine else xo
        return hall.at[at, c, pl.ds(first * CR + (n - 2) * (size // 2), size // 2)]

    def hx_copy(g, n):
        ref = hx_refs(g, n, True)
        return remote(ref, ref, hx_s.at[g, n], hx_r.at[g, n], dev((xr, xl)[n % 2], y, z, c))

    def hx_wait(g, n):
        ref = hx_refs(g, n, False)
        remote(ref, ref, hx_s.at[g, n], hx_r.at[g, n], dev(xr, y, z, c)).wait_recv()

    def hc_copy(g, n):
        ref = hall.at[(x, xl, xr, xo)[n], c, group_rows(g)]
        return remote(ref, ref, hc_s.at[g, n], hc_r.at[g, n], other_core)

    def hc_wait(g, n):
        ref = hall.at[(x, xl, xr, xo)[n], o, group_rows(g)]
        remote(ref, ref, hc_s.at[g, n], hc_r.at[g, n], other_core).wait_recv()

    def relay_hidden(g):
        for n in range(2):
            hx_wait(g, n)
            hx_copy(g, 2 + n).start()
            hc_copy(g, 1 + n).start()

    def last_hidden(g):
        hx_wait(g, 2)
        hx_wait(g, 3)
        hc_copy(g, 3).start()

    def hess_cols(n):
        at = (x, xl, xr, xo)[n]
        return pl.ds(pl.multiple_of(at * 2 * FB, 2 * FB), 2 * FB)

    def hess_part(g, n):
        hc_wait(g, n)
        at = (x, xl, xr, xo)[n]
        r = group_rows(g)
        right = jnp.concatenate([hall[at, 0, r], hall[at, 1, r]], axis=1)
        got = lax.dot_general(hall[x, c, r], right, (((0,), (0,)), ((), ())), preferred_element_type=F32)
        cols = hess_cols(n)
        if g > 0:
            got = hess[:, cols] + got
        hess[:, cols] = got * scale_out if g == len(GROUPS) - 1 else got

    def out_remote(n):
        cols = hess_cols(n)
        return remote(hess.at[:, cols], hess_out.at[:, cols], f_s.at[n], f_r.at[n], owner)

    def out_local(n):
        cols = hess_cols(n)
        return pltpu.make_async_copy(hess.at[:, cols], hess_out.at[:, cols], f_r.at[n])

    def out_start(n):
        @pl.when(c != l)
        def _():
            out_remote(n).start()

        @pl.when(c == l)
        def _():
            out_local(n).start()

    def restore():
        for g in range(len(GROUPS)):
            ho_local(g).wait()
        r = lax.broadcasted_iota(jnp.int32, (NZ * NH * RB, NZ * NH * RB), 0)
        q = lax.broadcasted_iota(jnp.int32, (NZ * NH * RB, NZ * NH * RB), 1)
        y_at = ((r // 32) % 4) * 2 + r // 128
        y_rank = rank_of((y_at + NY - (yh * 2 + c)) % NY)
        z_rank = rank_of(((r // 4) % NZ + NZ - z) % NZ)
        turn = jnp.where(q == z_rank * (NH * RB) + y_rank * 4 + r % 4, 1.0, 0.0).astype(BF16)
        for s in range(NX):
            block = jnp.concatenate([hown[j * CR + s * NH * RB : j * CR + (s + 1) * NH * RB] for j in range(NZ)], axis=0)
            hperm[s * 256 : (s + 1) * 256] = jnp.dot(turn, block, preferred_element_type=F32).astype(BF16)

    for piece in range(2):
        for way in range(2):
            y_send(0, way, piece).start()
    y_hop(0)
    y_hop(1)
    select(0)
    fill(0, 0, 3)
    stage_b(0)
    z_start(0)
    z_start(1)
    y_hop(2)
    fill(0, 3, NZ)
    w_start()
    stage_b(1)
    stage_c(0)
    y_hop(3)
    select(1)
    fill(1, 0, NZ)
    for n in range(2, AHEAD):
        z_start(n)
    stage_b(2)
    acts = {"B": stage_b, "C": stage_c, "D": stage_d, "F": finish_hidden, "R": relay_hidden, "L": last_hidden}
    for step in PLAN:
        act, n = step[0], int(step[1:])
        if act == "H":
            for m in range(4):
                hess_part(n, m)
        elif act == "E":
            hess_part(len(GROUPS) - 1, n)
            out_start(n)
        else:
            acts[act](n)
    restore()
    hidden_copy = pltpu.make_async_copy(hperm, hidden_out, in_s.at[0])
    hidden_copy.start()

    for n in range(2):
        core_copy(n).wait_send()
    for step, way, piece in y_all:
        y_send(step, way, piece).wait_send()
    w_wait_send()
    for h in range(NH):
        for j in range(1, NZ):
            z_copy(h, j).wait_send()
    for i in range(len(PIECES)):
        for n in range(4):
            x_copy(i, n).wait_send()
    for j in range(NZ):
        p_copy(j).wait_send()
    for g in range(len(GROUPS)):
        for n in range(4):
            hx_copy(g, n).wait_send()
            hc_copy(g, n).wait_send()

        @pl.when(c != l)
        def _():
            ho_remote(g).wait_send()

    for n in range(4):
        @pl.when(c != l)
        def _():
            out_remote(n).wait_send()

        out_local(n).wait()
    hidden_copy.wait()


def shards(codes, exponents, routes, gate_weight, up_weight):
    sem = pltpu.SemaphoreType.DMA
    hbm = pl.BlockSpec(memory_space=pl.ANY)
    scale_out = 1.0 / (TOK * NX * NY * NZ * 2 * routes.shape[1] // (NY * NZ))
    groups = len(GROUPS)
    hidden, hess = pl.pallas_call(
        functools.partial(kernel, scale_out),
        out_shape=(
            jax.ShapeDtypeStruct((SL, FB), BF16),
            jax.ShapeDtypeStruct((FB, NX * 2 * FB), F32),
        ),
        in_specs=[hbm] * 5,
        out_specs=(hbm, hbm),
        scratch_shapes=[
            pltpu.VMEM(codes.shape, BF16),
            pltpu.VMEM(exponents.shape, jnp.int32),
            pltpu.VMEM(routes.shape, jnp.int32),
            pltpu.VMEM((2 * BLK, TOK, LANES), F32),
            pltpu.VMEM((TOK, LANES), F32),
            pltpu.VMEM((BLK, TOK, LANES), F32),
            pltpu.VMEM((TOK, LANES), F32),
            pltpu.VMEM((NY, 1 + BLK, 2 * TOK, LANES), BF16),
            pltpu.VMEM((NZ * RB, 8 * TOK), BF16),
            pltpu.VMEM((NH, NZ, RB, HALF), BF16),
            pltpu.VMEM((NX, NZ, NH, RB, HALF), BF16),
            pltpu.VMEM((4, HALF, FB), BF16),
            pltpu.VMEM((2, SL, 2 * FB), F32),
            pltpu.VMEM((SL, 2 * FB), F32),
            pltpu.VMEM((NX, 2, SL, FB), BF16),
            pltpu.VMEM((SL, FB), BF16),
            pltpu.VMEM((SL, FB), BF16),
            pltpu.VMEM((FB, NX * 2 * FB), F32),
            sem((3,)),
            sem((2,)),
            sem((2,)),
            sem((4, 2, 2)),
            sem((4, 2, 2)),
            sem((NH, NZ)),
            sem((NH, NZ)),
            sem((len(PIECES), 4)),
            sem((len(PIECES), 4)),
            sem((2, 2)),
            sem((4,)),
            sem((NZ,)),
            sem((NZ,)),
            sem((groups, 4)),
            sem((groups, 4)),
            sem((groups, 4)),
            sem((groups, 4)),
            sem((groups,)),
            sem((groups,)),
            sem((4,)),
            sem((4,)),
        ],
        compiler_params=pltpu.CompilerParams(
            collective_id=0, has_side_effects=True, vmem_limit_bytes=60 * 1024 * 1024
        ),
        name="routed_stats",
    )(codes, exponents, routes, gate_weight[0], up_weight[0])
    return hidden[None], hess[None]


def solution(mesh):
    placed = (
        P(("dp", "expert"), None),
        P(("dp", "expert"), None),
        P(("dp", "expert"), None),
        P("expert", None, "dp"),
        P("expert", None, "dp"),
    )
    return jax.shard_map(
        shards,
        mesh=mesh,
        in_specs=placed,
        out_specs=(P("expert", None, "dp"), P("expert", "dp", None)),
        check_vma=False,
    )
```
